128 devices in a mesh: dp: 8 (over z, y_hi), tensor: 16 (over x, y_lo, core).
Axes of the slice: x: 4, y: 4 (y_hi: 2, y_lo: 2; y = y_hi * 2 + y_lo), z: 4, core: 2. Of those that a mesh axis runs over, the one named last changes fastest.
Arguments:
- hidden_train: bfloat16 [32, 1024, 28672], P('dp', None, 'tensor'), may hold values from -6 to 6
- outgrad_train: bfloat16 [32, 1024, 8192], P('dp', None, 'tensor'), may hold values from -6 to 6
- hidden_query: bfloat16 [8, 1024, 28672], P('dp', None, 'tensor'), may hold values from -6 to 6
- outgrad_query: bfloat16 [8, 1024, 8192], P('dp', None, 'tensor'), may hold values from -6 to 6
- proj_in: bfloat16 [28672, 64], P('tensor'), may hold values from -0.03125 to 0.03125
- proj_out: bfloat16 [8192, 64], P('tensor'), may hold values from -0.0625 to 0.0625
Outputs:
- train_grads: float32 [32, 4096], P('dp', 'tensor')
- scores: float32 [32, 8], P('dp')
The draws below stay inside these ranges and needn't reach their ends.
All inputs are finite; a program needn't handle non-finite values.
Results may differ from the reference program's by a relative error of at most 0.0003.
Values sent between devices are 32-bit elements; how exact they have to be, the bound alone decides.
A program may use at most 128 MiB of HBM per device.

```python
import jax
import jax.numpy as jnp
from jax import lax

D = 8192
FF = 28672
R = 64
LEN = 1024
TRAIN = 32
QUERIES = 8


def levels(rng, dims, cuts, smallest, top_value):
    loudness, own = 1.0, jax.random.fold_in(rng, 6)
    for dim, parts in cuts:
        draws = jnp.exp(jax.random.uniform(jax.random.fold_in(own, dim), (parts,), jnp.float32, smallest / len(cuts), top_value / len(cuts)))
        loudness = loudness * jnp.repeat(draws, dims[dim] // parts).reshape([-1 if axis == dim else 1 for axis in range(len(dims))])
    return loudness


def gaussian(rng, extent, width, bound, split=(), kind=jnp.bfloat16):
    drawn = jax.random.normal(rng, extent, jnp.float32) * width
    if len(split) > 0:
        drawn = levels(rng, extent, split, -0.22, 0.18) * drawn
    return jnp.clip(drawn, min=-bound, max=bound).astype(kind)


def setup_inputs(seed: int = 0) -> dict:
    key_list = jax.random.split(jax.random.key(seed), 7)
    return {
        "hidden_train": gaussian(key_list[0], (TRAIN, LEN, FF), 1.0, 6.0, ((0, 8), (2, 16))),
        "outgrad_train": gaussian(key_list[1], (TRAIN, LEN, D), 1.0, 6.0, ((0, 8), (2, 16))),
        "hidden_query": gaussian(key_list[2], (QUERIES, LEN, FF), 1.0, 6.0, ((0, 8), (2, 16))),
        "outgrad_query": gaussian(key_list[3], (QUERIES, LEN, D), 1.0, 6.0, ((0, 8), (2, 16))),
        "proj_in": gaussian(key_list[4], (FF, R), FF ** -0.5, 0.03125, ((0, 16),)),
        "proj_out": gaussian(key_list[5], (D, R), D ** -0.5, 0.0625, ((0, 16),)),
    }


def project(hidden, outgrad, proj_in, proj_out):
    seqs = hidden.shape[0]
    length = hidden.shape[1]
    first = jnp.dot(hidden.reshape(seqs * length, hidden.shape[2]), proj_in, preferred_element_type=jnp.float32)
    second = jnp.dot(outgrad.reshape(seqs * length, outgrad.shape[2]), proj_out, preferred_element_type=jnp.float32)
    first = first.reshape(seqs, length, R)
    second = second.reshape(seqs, length, R)
    outer = jnp.einsum('str,stk->srk', first, second, precision=lax.Precision.HIGHEST)
    outer = outer / jnp.sqrt(jnp.float32(LEN))
    return outer.reshape(seqs, R * R)

def reference(hidden_train, outgrad_train, hidden_query, outgrad_query, proj_in, proj_out):
    train_grads = project(hidden_train, outgrad_train, proj_in, proj_out)
    query_grads = project(hidden_query, outgrad_query, proj_in, proj_out)
    scores = jnp.dot(train_grads, query_grads.T, precision=lax.Precision.HIGHEST) / R
    return (train_grads, scores)
```

```python
import functools

import jax
import jax.numpy as jnp
from jax import lax
from jax.experimental import pallas as pl
from jax.experimental.pallas import tpu as pltpu
from jax.sharding import PartitionSpec as P

MESH = pl.DeviceIdType.MESH
HIGHEST = lax.Precision.HIGHEST
SEQS = 5
HALF = 512
OFFSETS = [
    (dx, dy, dc)
    for dx in (2, 1, 3, 0)
    for dy in (1, 0)
    for dc in (1, 0)
    if (dx, dy, dc) != (0, 0, 0)
]
PARTS = ((0, 320, "YX"), (320, 192, "XY"))
AFTER_CORE, AFTER_ONE, AFTER_TWO = 1, 4, 3
QUERY_STEP = 13


def kernel(
    ht, ot, hq, oq, pi, po, grads_ref, scores_ref,
    hb, ob, w, acc, cbuf, rbuf, mbuf, gsend, gbuf, qown, qbuf, sbuf,
    hbm_sem, core_ss, core_rs, ss, rs, g_ss, g_rs, q_ss, q_rs, s_ss, s_rs,
):
    t = lax.axis_index("tensor")
    group = lax.axis_index("dp")
    x, y, c = t // 4, (t // 2) % 2, t % 2

    def at(dx, dy, dc):
        xx = lax.rem(x + dx, 4)
        yy = 1 - y if dy else y
        cc = 1 - c if dc else c
        return {"tensor": (xx * 2 + yy) * 2 + cc}

    def row(v, m):
        return pl.multiple_of(v, m)

    loads = [
        pltpu.make_async_copy(pi, w.at[pl.ds(0, 64), pl.ds(0, 1792)], hbm_sem.at[0]),
        pltpu.make_async_copy(po, w.at[pl.ds(64, 64), pl.ds(1792, 512)], hbm_sem.at[1]),
    ]
    halves = [1 - c, c]
    for s in range(SEQS):
        for p in range(2):
            r = halves[p]
            i = 2 + (s * 2 + p) * 2
            h = hq.at[0, r] if s == 0 else ht.at[s - 1, r]
            o = oq.at[0, r] if s == 0 else ot.at[s - 1, r]
            here = pl.ds(p * HALF, HALF)
            loads.append(pltpu.make_async_copy(h, hb.at[s, here], hbm_sem.at[i]))
            loads.append(pltpu.make_async_copy(o, ob.at[s, here], hbm_sem.at[i + 1]))
    for load in loads:
        load.start()
    barrier = pltpu.get_barrier_semaphore()
    for off in OFFSETS:
        pl.semaphore_signal(barrier, inc=1, device_id=at(*off), device_id_type=MESH)
    for k in range(1, 8):
        pl.semaphore_signal(
            barrier, inc=1, device_id={"dp": lax.rem(group + k, 8)}, device_id_type=MESH
        )

    w[pl.ds(64, 64), pl.ds(0, 1792)] = jnp.zeros((64, 1792), jnp.bfloat16)
    w[pl.ds(0, 64), pl.ds(1792, 512)] = jnp.zeros((64, 512), jnp.bfloat16)
    loads[0].wait()
    loads[1].wait()

    def remote(src, dst, send, recv, device):
        return pltpu.make_async_remote_copy(
            src_ref=src, dst_ref=dst, send_sem=send, recv_sem=recv,
            device_id=device, device_id_type=MESH,
        )

    def compute(k):
        s, p = k // 2, k % 2
        r = pl.ds(row(p * HALF, HALF), HALF)
        i = 2 + k * 2
        pltpu.make_async_copy(hq.at[0, 0], hb.at[s, r], hbm_sem.at[i]).wait()
        pltpu.make_async_copy(oq.at[0, 0], ob.at[s, r], hbm_sem.at[i + 1]).wait()
        dims = (((1,), (1,)), ((), ()))
        total = lax.dot_general(
            hb[s, r], w[:, 0:1792], dims, preferred_element_type=jnp.float32
        )
        total = total + lax.dot_general(
            ob[s, r], w[:, 1792:2304], dims, preferred_element_type=jnp.float32
        )
        acc[s, r] = total

    def core_copy(s):
        return remote(
            acc.at[s, pl.ds(0, HALF)], cbuf.at[s], core_ss.at[s], core_rs.at[s], at(0, 0, 1)
        )

    def along(part, n):
        first, rows, way = part
        base = HALF + first
        if way == "YX":
            if n == 0:
                return "y", rows // 2, base, first
            return "x", rows // 8, base + y * (rows // 2), first + rows // 2
        if n == 0:
            return "x", rows // 4, base, first
        return "y", rows // 8, base + x * (rows // 4), first + 3 * (rows // 4)

    def copies(s, j, n):
        way, share, lo, off = along(PARTS[j], n)
        if way == "y":
            hops, sem = (0,), 0
        else:
            hops, sem = (2, 1, 3), 1
        found = []
        for k, dx in enumerate(hops):
            to = lax.rem(x + dx, 4) if way == "x" else 1 - y
            found.append(remote(
                acc.at[s, pl.ds(row(lo + to * share, 8), share)],
                rbuf.at[s, pl.ds(off + k * share, share)],
                ss.at[s, j, sem + k], rs.at[s, j, sem + k],
                at(dx, 0, 0) if way == "x" else at(0, 1, 0),
            ))
        return found

    def arrive(s, j, n):
        way, share, lo, off = along(PARTS[j], n)
        arrived = copies(s, j, n)
        for copy in arrived:
            copy.wait_recv()
        mine = pl.ds(row(lo + (x if way == "x" else y) * share, 8), share)
        total = acc[s, mine]
        for k in range(len(arrived)):
            total = total + rbuf[s, pl.ds(off + k * share, share)]
        return mine, total

    lane = lax.broadcasted_iota(jnp.int32, (16, 128), 1)

    def partial_grad(s):
        both = jnp.concatenate([arrive(s, j, 1)[1] for j in range(len(PARTS))], axis=0)
        wide = lax.broadcasted_iota(jnp.int32, both.shape, 1)
        twice = jnp.where(wide < 64, pltpu.roll(both, 64, 1), both)
        outer = lax.dot_general(
            both, twice, (((0,), (0,)), ((), ())), precision=HIGHEST,
            preferred_element_type=jnp.float32,
        )
        mbuf[...] = outer[0:64]
        for h in range(2):
            even = mbuf[pl.ds(2 * h, 16, stride=4)]
            odd = mbuf[pl.ds(2 * h + 1, 16, stride=4)]
            gsend[jnp.minimum(s, 1), h, pl.ds(s, 16, stride=8)] = jnp.where(lane < 64, even, odd)

    def spread(slot):
        found = []
        for k, off in enumerate(OFFSETS):
            to = at(*off)
            found.append(remote(
                gsend.at[slot, :, pl.ds(row(to["tensor"] * 8, 8), 8)], gbuf.at[slot, k],
                g_ss.at[slot, k], g_rs.at[slot, k], to,
            ))
        return found

    def collect(slot):
        for copy in spread(slot):
            copy.wait_recv()
        total = gsend[slot, :, pl.ds(row(t * 8, 8), 8)]
        for k in range(15):
            total = total + gbuf[slot, k]
        return total * (1.0 / 32.0)

    def query_copies():
        return [
            remote(
                qown, qbuf.at[group], q_ss.at[k - 1], q_rs.at[k - 1],
                {"dp": lax.rem(group + k, 8)},
            )
            for k in range(1, 8)
        ]

    def score_copies():
        return [
            remote(sbuf.at[t], sbuf.at[t], s_ss.at[k], s_rs.at[k], at(*off))
            for k, off in enumerate(OFFSETS)
        ]

    def when_due(k, lag, act):
        s2 = k - 1 - lag

        @pl.when((s2 >= 0) & (s2 % 2 == 0) & (s2 < 2 * SEQS))
        def _():
            act(s2 // 2)

    def after_core(s):
        core_copy(s).wait_recv()
        own = pl.ds(HALF, HALF)
        acc[s, own] = acc[s, own] + cbuf[s]
        for j in range(len(PARTS)):
            for copy in copies(s, j, 0):
                copy.start()

    def after_one(s):
        for j in range(len(PARTS)):
            mine, total = arrive(s, j, 0)
            acc[s, mine] = total
            for copy in copies(s, j, 1):
                copy.start()

    def after_two(s):
        partial_grad(s)

        @pl.when(s == 0)
        def _():
            for copy in spread(0):
                copy.start()

    gsend[...] = jnp.zeros_like(gsend)

    def half_step(k, carry):
        @pl.when(k < 2 * SEQS)
        def _():
            compute(k)

        @pl.when(k == 0)
        def _():
            pl.semaphore_wait(barrier, 22)

        @pl.when((k % 2 == 0) & (k < 2 * SEQS))
        def _():
            core_copy(k // 2).start()

        when_due(k, AFTER_CORE, after_core)
        when_due(k, AFTER_CORE + AFTER_ONE, after_one)
        when_due(k, AFTER_CORE + AFTER_ONE + AFTER_TWO, after_two)

        @pl.when(k == QUERY_STEP)
        def _():
            qown[...] = collect(0)
            qbuf[group] = qown[...]
            for copy in query_copies():
                copy.start()

        return carry

    lax.fori_loop(0, 2 * SEQS + AFTER_CORE + AFTER_ONE + AFTER_TWO, half_step, 0)

    for copy in spread(1):
        copy.start()
    grads = collect(1)
    for copy in query_copies():
        copy.wait_recv()
    part = jnp.zeros((8, 8), jnp.float32)
    for h in range(2):
        queries = jnp.concatenate([qbuf[k, h, 0:1] for k in range(8)], axis=0)
        part = part + lax.dot_general(
            grads[h], queries, (((1,), (1,)), ((), ())), precision=HIGHEST,
            preferred_element_type=jnp.float32,
        )
    sbuf[t, :, 0:8] = part
    for copy in score_copies():
        copy.start()
    for h in range(2):
        grads_ref[:, pl.ds(h * 128, 128)] = grads[h, 1:5]

    def sent(s, carry):
        core_copy(s).wait_send()
        for j in range(len(PARTS)):
            for n in range(2):
                for copy in copies(s, j, n):
                    copy.wait_send()
        return carry

    lax.fori_loop(0, SEQS, sent, 0)
    for copy in spread(0) + spread(1) + query_copies():
        copy.wait_send()
    for copy in score_copies():
        copy.wait_recv()
    total = sbuf[0]
    for k in range(1, 16):
        total = total + sbuf[k]
    scores_ref[...] = total[1:5, 0:8] * (1.0 / 64.0)
    for copy in score_copies():
        copy.wait_send()


def on_device(hidden_train, outgrad_train, hidden_query, outgrad_query, proj_in, proj_out):
    anywhere = pl.BlockSpec(memory_space=pl.ANY)
    vmem = pl.BlockSpec(memory_space=pltpu.VMEM)
    f32, bf16 = jnp.float32, jnp.bfloat16
    dma = pltpu.SemaphoreType.DMA
    return pl.pallas_call(
        kernel,
        out_shape=(jax.ShapeDtypeStruct((4, 256), f32), jax.ShapeDtypeStruct((4, 8), f32)),
        in_specs=[anywhere] * 6,
        out_specs=(vmem, vmem),
        scratch_shapes=[
            pltpu.VMEM((SEQS, 1024, 1792), bf16),
            pltpu.VMEM((SEQS, 1024, 512), bf16),
            pltpu.VMEM((128, 2304), bf16),
            pltpu.VMEM((SEQS, 1024, 128), f32),
            pltpu.VMEM((SEQS, HALF, 128), f32),
            pltpu.VMEM((SEQS, HALF, 128), f32),
            pltpu.VMEM((64, 128), f32),
            pltpu.VMEM((2, 2, 128, 128), f32),
            pltpu.VMEM((2, 15, 2, 8, 128), f32),
            pltpu.VMEM((2, 8, 128), f32),
            pltpu.VMEM((8, 2, 8, 128), f32),
            pltpu.VMEM((16, 8, 128), f32),
            dma((2 + SEQS * 4,)),
            dma((SEQS,)),
            dma((SEQS,)),
            dma((SEQS, 2, 4)),
            dma((SEQS, 2, 4)),
            dma((2, 15)),
            dma((2, 15)),
            dma((7,)),
            dma((7,)),
            dma((15,)),
            dma((15,)),
        ],
        compiler_params=pltpu.CompilerParams(
            collective_id=0, has_side_effects=True, vmem_limit_bytes=56 * 2**20
        ),
    )(
        *(
            a.reshape(a.shape[0], 2, HALF, a.shape[2])
            for a in (hidden_train, outgrad_train, hidden_query, outgrad_query)
        ),
        proj_in.T,
        proj_out.T,
    )


def solution(mesh):
    placed = (
        P("dp", None, "tensor"),
        P("dp", None, "tensor"),
        P("dp", None, "tensor"),
        P("dp", None, "tensor"),
        P("tensor", None),
        P("tensor", None),
    )
    return jax.shard_map(
        on_device,
        mesh=mesh,
        in_specs=placed,
        out_specs=(P("dp", "tensor"), P("dp", None)),
        check_vma=False,
    )
```

```python
import jax
import jax.numpy as jnp
from jax import lax
from jax.experimental import pallas as pl
from jax.experimental.pallas import tpu as pltpu
from jax.sharding import PartitionSpec as P

MESH = pl.DeviceIdType.MESH
HIGHEST = lax.Precision.HIGHEST
SEQS, CHUNKS, ROWS, HALF = 5, 10, 512, 256
OWN = HALF // 8
OFFSETS = [
    (dx, dy, dc)
    for dx in (2, 1, 3, 0)
    for dy in (1, 0)
    for dc in (1, 0)
    if (dx, dy, dc) != (0, 0, 0)
]
WAYS = ("YX", "XY")
TO_CORE, TO_ONE, TO_TWO = 1, 5, 9
QUERY_STEP = 15


def kernel(
    ht, ot, hq, oq, pi, po, out_ref,
    hb, ob, w, acc, cbuf, rbuf, fin, mbuf, gsend, gbuf, qbuf, sbuf,
    hbm_sem, core_ss, core_rs, ss, rs, g_ss, g_rs, q_ss, q_rs, s_ss, s_rs,
):
    t = lax.axis_index("tensor")
    group = lax.axis_index("dp")
    x, y, c = t // 4, (t // 2) % 2, t % 2

    def at(dx, dy, dc):
        xx = lax.rem(x + dx, 4)
        yy = 1 - y if dy else y
        cc = 1 - c if dc else c
        return {"tensor": (xx * 2 + yy) * 2 + cc}

    def row(v, m):
        return pl.multiple_of(v, m)

    loads = [
        pltpu.make_async_copy(pi, w.at[pl.ds(0, 64), pl.ds(0, 1792)], hbm_sem.at[0]),
        pltpu.make_async_copy(po, w.at[pl.ds(64, 64), pl.ds(1792, 512)], hbm_sem.at[1]),
    ]
    for k in range(CHUNKS):
        for p, side in enumerate((1 - c, c)):
            here = pl.ds(p * HALF, HALF)
            i = 2 + (k * 2 + p) * 2
            h = hq.at[0, k, side] if k < 2 else ht.at[k // 2 - 1, k % 2, side]
            o = oq.at[0, k, side] if k < 2 else ot.at[k // 2 - 1, k % 2, side]
            loads.append(pltpu.make_async_copy(h, hb.at[k, here], hbm_sem.at[i]))
            loads.append(pltpu.make_async_copy(o, ob.at[k, here], hbm_sem.at[i + 1]))
    for load in loads:
        load.start()
    barrier = pltpu.get_barrier_semaphore()
    for off in OFFSETS:
        pl.semaphore_signal(barrier, inc=1, device_id=at(*off), device_id_type=MESH)
    for k in range(1, 8):
        pl.semaphore_signal(
            barrier, inc=1, device_id={"dp": lax.rem(group + k, 8)}, device_id_type=MESH
        )
    w[pl.ds(64, 64), pl.ds(0, 1792)] = jnp.zeros((64, 1792), jnp.bfloat16)
    w[pl.ds(0, 64), pl.ds(1792, 512)] = jnp.zeros((64, 512), jnp.bfloat16)
    gsend[...] = jnp.zeros_like(gsend)
    loads[0].wait()
    loads[1].wait()

    def remote(src, dst, send, recv, device):
        return pltpu.make_async_remote_copy(
            src_ref=src, dst_ref=dst, send_sem=send, recv_sem=recv,
            device_id=device, device_id_type=MESH,
        )

    def compute(k):
        for p in range(2):
            i = 2 + (k * 2 + p) * 2
            here = pl.ds(p * HALF, HALF)
            pltpu.make_async_copy(hq.at[0, 0, 0], hb.at[k, here], hbm_sem.at[i]).wait()
            pltpu.make_async_copy(oq.at[0, 0, 0], ob.at[k, here], hbm_sem.at[i + 1]).wait()
        dims = (((1,), (1,)), ((), ()))
        total = lax.dot_general(
            hb[k], w[:, 0:1792], dims, preferred_element_type=jnp.float32
        )
        total = total + lax.dot_general(
            ob[k], w[:, 1792:2304], dims, preferred_element_type=jnp.float32
        )
        acc[k] = total

    def core_copy(k):
        return remote(
            acc.at[k, pl.ds(0, HALF)], cbuf.at[k], core_ss.at[k], core_rs.at[k], at(0, 0, 1)
        )

    def along(way, n):
        if way == "YX":
            if n == 0:
                return "y", HALF // 2, HALF, 0
            return "x", OWN, HALF + y * (HALF // 2), HALF // 2
        if n == 0:
            return "x", HALF // 4, HALF, 0
        return "y", OWN, HALF + x * (HALF // 4), 3 * (HALF // 4)

    def copies(k, way, n):
        axis, share, lo, off = along(way, n)
        if axis == "y":
            return [remote(
                acc.at[k, pl.ds(row(lo + (1 - y) * share, 8), share)],
                rbuf.at[k, pl.ds(off, share)], ss.at[k, 0], rs.at[k, 0], at(0, 1, 0),
            )]
        return [
            remote(
                acc.at[k, pl.ds(row(lo + lax.rem(x + dx, 4) * share, 8), share)],
                rbuf.at[k, pl.ds(off + q * share, share)],
                ss.at[k, 1 + q], rs.at[k, 1 + q], at(dx, 0, 0),
            )
            for q, dx in enumerate((2, 1, 3))
        ]

    def arrive(k, way, n):
        arrived = copies(k, way, n)
        for copy in arrived:
            copy.wait_recv()
        axis, share, lo, off = along(way, n)
        lo = lo + (x if axis == "x" else y) * share
        mine = pl.ds(row(lo, 8), share)
        total = acc[k, mine]
        for q in range(len(arrived)):
            total = total + rbuf[k, pl.ds(off + q * share, share)]
        return mine, total

    lane = lax.broadcasted_iota(jnp.int32, (16, 128), 1)

    def partial_grad(s):
        both = fin[pl.ds(row(s * 2 * OWN, 8), 2 * OWN)]
        wide = lax.broadcasted_iota(jnp.int32, both.shape, 1)
        twice = jnp.where(wide < 64, pltpu.roll(both, 64, 1), both)
        outer = lax.dot_general(
            both, twice, (((0,), (0,)), ((), ())), precision=HIGHEST,
            preferred_element_type=jnp.float32,
        )
        mbuf[...] = outer[0:64]
        for h in range(2):
            even = mbuf[pl.ds(2 * h, 16, stride=4)]
            odd = mbuf[pl.ds(2 * h + 1, 16, stride=4)]
            first = h * 4 + jnp.maximum(s - 1, 0)
            gsend[jnp.minimum(s, 1), pl.ds(first, 16, stride=8)] = jnp.where(lane < 64, even, odd)

    def spread(slot):
        found = []
        for q, off in enumerate(OFFSETS):
            to = at(*off)
            found.append(remote(
                gsend.at[slot, pl.ds(row(to["tensor"] * 8, 8), 8)], gbuf.at[slot, q],
                g_ss.at[slot, q], g_rs.at[slot, q], to,
            ))
        return found

    def collect(slot):
        for copy in spread(slot):
            copy.wait_recv()
        total = gsend[slot, pl.ds(row(t * 8, 8), 8)]
        for q in range(15):
            total = total + gbuf[slot, q]
        return total * (1.0 / 32.0)

    def query_copies():
        return [
            remote(
                qbuf.at[group], qbuf.at[group], q_ss.at[q - 1], q_rs.at[q - 1],
                {"dp": lax.rem(group + q, 8)},
            )
            for q in range(1, 8)
        ]

    def score_copies():
        return [
            remote(sbuf.at[t], sbuf.at[t], s_ss.at[q], s_rs.at[q], at(*off))
            for q, off in enumerate(OFFSETS)
        ]

    def when_chunk(k, act):
        for p, way in enumerate(WAYS):
            pl.when((k >= 0) & (k < CHUNKS) & (lax.rem(k, 2) == p))(lambda way=way: act(k, way))

    def start(found):
        for copy in found:
            copy.start()

    def sum_core(k):
        core_copy(k).wait_recv()
        own = pl.ds(HALF, HALF)
        acc[k, own] = acc[k, own] + cbuf[k]

    def first_sum(k, way):
        mine, total = arrive(k, way, 0)
        acc[k, mine] = total
        start(copies(k, way, 1))

    def last_sum(k, way):
        fin[pl.ds(row(k * OWN, 8), OWN)] = arrive(k, way, 1)[1]

    def grads_due(k):
        @pl.when((k >= 0) & (k < CHUNKS) & (lax.rem(k, 2) == 1))
        def _():
            partial_grad(k // 2)

        @pl.when(k == 1)
        def _():
            start(spread(0))

    def step(n, carry):
        @pl.when(n < CHUNKS)
        def _():
            compute(n)

        @pl.when(n == 0)
        def _():
            pl.semaphore_wait(barrier, 22)

        @pl.when(n < CHUNKS)
        def _():
            core_copy(n).start()

        k = n - TO_CORE

        @pl.when((k >= 0) & (k < CHUNKS))
        def _():
            sum_core(k)

        when_chunk(k, lambda k, way: start(copies(k, way, 0)))
        when_chunk(n - TO_ONE, first_sum)
        when_chunk(n - TO_TWO, last_sum)
        grads_due(n - TO_TWO)

        @pl.when(n == QUERY_STEP)
        def _():
            qbuf[group] = collect(0)
            start(query_copies())

        return carry

    lax.fori_loop(0, CHUNKS + TO_TWO, step, 0)

    start(spread(1))
    grads = collect(1)
    for copy in query_copies():
        copy.wait_recv()
    parts = []
    for h in range(2):
        queries = jnp.concatenate([qbuf[q, h * 4 : h * 4 + 1] for q in range(8)], axis=0)
        parts.append(lax.dot_general(
            grads, queries, (((1,), (1,)), ((), ())), precision=HIGHEST,
            preferred_element_type=jnp.float32,
        ))
    sbuf[t, 0:4, 0:8] = parts[0][0:4] + parts[1][4:8]
    start(score_copies())
    out_ref[0] = grads

    def sent(s, carry):
        for p, way in enumerate(WAYS):
            k = s * 2 + p
            core_copy(k).wait_send()
            for copy in copies(k, way, 0) + copies(k, way, 1):
                copy.wait_send()
        return carry

    lax.fori_loop(0, SEQS, sent, 0)
    for copy in spread(0) + spread(1) + query_copies():
        copy.wait_send()
    for copy in score_copies():
        copy.wait_recv()
    total = sbuf[0]
    for q in range(1, 16):
        total = total + sbuf[q]
    out_ref[1] = total * (1.0 / 64.0)
    for copy in score_copies():
        copy.wait_send()


def unpack(packed, grads_ref, scores_ref):
    for h in range(2):
        grads_ref[:, pl.ds(h * 128, 128)] = packed[0, h * 4 : h * 4 + 4]
    scores_ref[...] = packed[1, 0:4, 0:8]


def on_device(hidden_train, outgrad_train, hidden_query, outgrad_query, proj_in, proj_out):
    anywhere = pl.BlockSpec(memory_space=pl.ANY)
    vmem = pl.BlockSpec(memory_space=pltpu.VMEM)
    f32, bf16 = jnp.float32, jnp.bfloat16
    dma = pltpu.SemaphoreType.DMA
    packed = pl.pallas_call(
        kernel,
        out_shape=jax.ShapeDtypeStruct((2, 8, 128), f32),
        in_specs=[anywhere] * 6,
        out_specs=vmem,
        scratch_shapes=[
            pltpu.VMEM((CHUNKS, ROWS, 1792), bf16),
            pltpu.VMEM((CHUNKS, ROWS, 512), bf16),
            pltpu.VMEM((128, 2304), bf16),
            pltpu.VMEM((CHUNKS, ROWS, 128), f32),
            pltpu.VMEM((CHUNKS, HALF, 128), f32),
            pltpu.VMEM((CHUNKS, HALF, 128), f32),
            pltpu.VMEM((CHUNKS * OWN, 128), f32),
            pltpu.VMEM((64, 128), f32),
            pltpu.VMEM((2, 128, 128), f32),
            pltpu.VMEM((2, 15, 8, 128), f32),
            pltpu.VMEM((8, 8, 128), f32),
            pltpu.VMEM((16, 8, 128), f32),
            dma((2 + CHUNKS * 4,)),
            dma((CHUNKS,)),
            dma((CHUNKS,)),
            dma((CHUNKS, 8)),
            dma((CHUNKS, 8)),
            dma((2, 15)),
            dma((2, 15)),
            dma((7,)),
            dma((7,)),
            dma((15,)),
            dma((15,)),
        ],
        compiler_params=pltpu.CompilerParams(
            collective_id=0, has_side_effects=True, vmem_limit_bytes=56 * 2**20
        ),
    )(
        *(
            a.reshape(a.shape[0], 2, 2, HALF, a.shape[2])
            for a in (hidden_train, outgrad_train, hidden_query, outgrad_query)
        ),
        proj_in.T,
        proj_out.T,
    )
    return pl.pallas_call(
        unpack,
        out_shape=(jax.ShapeDtypeStruct((4, 256), f32), jax.ShapeDtypeStruct((4, 8), f32)),
        in_specs=[vmem],
        out_specs=(vmem, vmem),
    )(packed)


def solution(mesh):
    placed = (
        P("dp", None, "tensor"),
        P("dp", None, "tensor"),
        P("dp", None, "tensor"),
        P("dp", None, "tensor"),
        P("tensor", None),
        P("tensor", None),
    )
    return jax.shard_map(
        on_device,
        mesh=mesh,
        in_specs=placed,
        out_specs=(P("dp", "tensor"), P("dp", None)),
        check_vma=False,
    )
```

```python
import jax
import jax.numpy as jnp
from jax import lax
from jax.experimental import pallas as pl
from jax.experimental.pallas import tpu as pltpu
from jax.sharding import PartitionSpec as P

MESH = pl.DeviceIdType.MESH
HIGHEST = lax.Precision.HIGHEST
SEQS, CHUNKS, ROWS, HALF = 5, 10, 512, 256
OWN = HALF // 8
OFFSETS = [
    (dx, dy, dc)
    for dx in (2, 1, 3, 0)
    for dy in (1, 0)
    for dc in (1, 0)
    if (dx, dy, dc) != (0, 0, 0)
]
WAYS = ("YX", "XY")
TO_CORE, TO_ONE, TO_TWO = 1, 5, 9
QUERY_STEP = 15


def kernel(
    ht, ot, hq, oq, pi, po, out_ref,
    hb, ob, w, acc, cbuf, rbuf, fin, mbuf, gsend, gbuf, qbuf, sbuf,
    hbm_sem, core_ss, core_rs, ss, rs, g_ss, g_rs, q_ss, q_rs, s_ss, s_rs,
):
    t = lax.axis_index("tensor")
    group = lax.axis_index("dp")
    x, y, c = t // 4, (t // 2) % 2, t % 2

    def at(dx, dy, dc):
        xx = lax.rem(x + dx, 4)
        yy = 1 - y if dy else y
        cc = 1 - c if dc else c
        return {"tensor": (xx * 2 + yy) * 2 + cc}

    def row(v, m):
        return pl.multiple_of(v, m)

    barrier = pltpu.get_barrier_semaphore()
    for k in range(1, 8):
        pl.semaphore_signal(
            barrier, inc=1, device_id={"dp": lax.rem(group + k, 8)}, device_id_type=MESH
        )
    for off in OFFSETS:
        pl.semaphore_signal(barrier, inc=1, device_id=at(*off), device_id_type=MESH)
    loads = [
        pltpu.make_async_copy(pi, w.at[pl.ds(0, 64), pl.ds(0, 1792)], hbm_sem.at[0]),
        pltpu.make_async_copy(po, w.at[pl.ds(64, 64), pl.ds(1792, 512)], hbm_sem.at[1]),
    ]
    for k in range(CHUNKS):
        for p, side in enumerate((1 - c, c)):
            here = pl.ds(p * HALF, HALF)
            i = 2 + (k * 2 + p) * 2
            h = hq.at[0, k, side] if k < 2 else ht.at[k // 2 - 1, k % 2, side]
            o = oq.at[0, k, side] if k < 2 else ot.at[k // 2 - 1, k % 2, side]
            loads.append(pltpu.make_async_copy(h, hb.at[k, here], hbm_sem.at[i]))
            loads.append(pltpu.make_async_copy(o, ob.at[k, here], hbm_sem.at[i + 1]))
    for load in loads:
        load.start()
    w[pl.ds(64, 64), pl.ds(0, 1792)] = jnp.zeros((64, 1792), jnp.bfloat16)
    w[pl.ds(0, 64), pl.ds(1792, 512)] = jnp.zeros((64, 512), jnp.bfloat16)
    gsend[...] = jnp.zeros_like(gsend)
    loads[0].wait()
    loads[1].wait()

    def remote(src, dst, send, recv, device):
        return pltpu.make_async_remote_copy(
            src_ref=src, dst_ref=dst, send_sem=send, recv_sem=recv,
            device_id=device, device_id_type=MESH,
        )

    def compute(k):
        for p in range(2):
            i = 2 + (k * 2 + p) * 2
            here = pl.ds(p * HALF, HALF)
            pltpu.make_async_copy(hq.at[0, 0, 0], hb.at[k, here], hbm_sem.at[i]).wait()
            pltpu.make_async_copy(oq.at[0, 0, 0], ob.at[k, here], hbm_sem.at[i + 1]).wait()
        dims = (((1,), (1,)), ((), ()))
        total = lax.dot_general(
            hb[k], w[:, 0:1792], dims, preferred_element_type=jnp.float32
        )
        total = total + lax.dot_general(
            ob[k], w[:, 1792:2304], dims, preferred_element_type=jnp.float32
        )
        acc[k] = total

    def core_copy(k):
        return remote(
            acc.at[k, pl.ds(0, HALF)], cbuf.at[k], core_ss.at[k], core_rs.at[k], at(0, 0, 1)
        )

    def along(way, n):
        if way == "YX":
            if n == 0:
                return "y", HALF // 2, HALF, 0
            return "x", OWN, HALF + y * (HALF // 2), HALF // 2
        if n == 0:
            return "x", HALF // 4, HALF, 0
        return "y", OWN, HALF + x * (HALF // 4), 3 * (HALF // 4)

    def copies(k, way, n):
        axis, share, lo, off = along(way, n)
        if axis == "y":
            return [remote(
                acc.at[k, pl.ds(row(lo + (1 - y) * share, 8), share)],
                rbuf.at[k, pl.ds(off, share)], ss.at[k, 0], rs.at[k, 0], at(0, 1, 0),
            )]
        return [
            remote(
                acc.at[k, pl.ds(row(lo + lax.rem(x + dx, 4) * share, 8), share)],
                rbuf.at[k, pl.ds(off + q * share, share)],
                ss.at[k, 1 + q], rs.at[k, 1 + q], at(dx, 0, 0),
            )
            for q, dx in enumerate((2, 1, 3))
        ]

    def arrive(k, way, n):
        arrived = copies(k, way, n)
        for copy in arrived:
            copy.wait_recv()
        axis, share, lo, off = along(way, n)
        lo = lo + (x if axis == "x" else y) * share
        mine = pl.ds(row(lo, 8), share)
        total = acc[k, mine]
        for q in range(len(arrived)):
            total = total + rbuf[k, pl.ds(off + q * share, share)]
        return mine, total

    lane = lax.broadcasted_iota(jnp.int32, (16, 128), 1)

    def partial_grad(s):
        both = fin[pl.ds(row(s * 2 * OWN, 8), 2 * OWN)]
        wide = lax.broadcasted_iota(jnp.int32, both.shape, 1)
        twice = jnp.where(wide < 64, pltpu.roll(both, 64, 1), both)
        outer = lax.dot_general(
            both, twice, (((0,), (0,)), ((), ())), precision=HIGHEST,
            preferred_element_type=jnp.float32,
        )
        mbuf[...] = outer[0:64]
        for h in range(2):
            even = mbuf[pl.ds(2 * h, 16, stride=4)]
            odd = mbuf[pl.ds(2 * h + 1, 16, stride=4)]
            first = h * 4 + jnp.maximum(s - 1, 0)
            gsend[jnp.minimum(s, 1), pl.ds(first, 16, stride=8)] = jnp.where(lane < 64, even, odd)

    def spread(slot):
        found = []
        for q, off in enumerate(OFFSETS):
            to = at(*off)
            found.append(remote(
                gsend.at[slot, pl.ds(row(to["tensor"] * 8, 8), 8)], gbuf.at[slot, q],
                g_ss.at[slot, q], g_rs.at[slot, q], to,
            ))
        return found

    def collect(slot):
        for copy in spread(slot):
            copy.wait_recv()
        total = gsend[slot, pl.ds(row(t * 8, 8), 8)]
        for q in range(15):
            total = total + gbuf[slot, q]
        return total * (1.0 / 32.0)

    def query_copies():
        return [
            remote(
                qbuf.at[group], qbuf.at[group], q_ss.at[q - 1], q_rs.at[q - 1],
                {"dp": lax.rem(group + q, 8)},
            )
            for q in range(1, 8)
        ]

    def score_copies():
        return [
            remote(sbuf.at[t], sbuf.at[t], s_ss.at[q], s_rs.at[q], at(*off))
            for q, off in enumerate(OFFSETS)
        ]

    def when_chunk(k, act):
        for p, way in enumerate(WAYS):
            pl.when((k >= 0) & (k < CHUNKS) & (lax.rem(k, 2) == p))(lambda way=way: act(k, way))

    def start(found):
        for copy in found:
            copy.start()

    def sum_core(k):
        core_copy(k).wait_recv()
        own = pl.ds(HALF, HALF)
        acc[k, own] = acc[k, own] + cbuf[k]

    def first_sum(k, way):
        mine, total = arrive(k, way, 0)
        acc[k, mine] = total
        start(copies(k, way, 1))

    def last_sum(k, way):
        fin[pl.ds(row(k * OWN, 8), OWN)] = arrive(k, way, 1)[1]

    def grads_due(k):
        @pl.when((k >= 0) & (k < CHUNKS) & (lax.rem(k, 2) == 1))
        def _():
            partial_grad(k // 2)

        @pl.when(k == 1)
        def _():
            start(spread(0))

    def step(n, carry):
        @pl.when(n < CHUNKS)
        def _():
            compute(n)

        @pl.when(n == 0)
        def _():
            pl.semaphore_wait(barrier, 22)

        @pl.when(n < CHUNKS)
        def _():
            core_copy(n).start()

        k = n - TO_CORE

        @pl.when((k >= 0) & (k < CHUNKS))
        def _():
            sum_core(k)

        when_chunk(k, lambda k, way: start(copies(k, way, 0)))
        when_chunk(n - TO_ONE, first_sum)
        when_chunk(n - TO_TWO, last_sum)
        grads_due(n - TO_TWO)

        @pl.when(n == QUERY_STEP)
        def _():
            qbuf[group] = collect(0)
            start(query_copies())

        return carry

    lax.fori_loop(0, CHUNKS + TO_TWO, step, 0)

    start(spread(1))
    grads = collect(1)
    for copy in query_copies():
        copy.wait_recv()
    parts = []
    for h in range(2):
        queries = jnp.concatenate([qbuf[q, h * 4 : h * 4 + 1] for q in range(8)], axis=0)
        parts.append(lax.dot_general(
            grads, queries, (((1,), (1,)), ((), ())), precision=HIGHEST,
            preferred_element_type=jnp.float32,
        ))
    sbuf[t, 0:4, 0:8] = parts[0][0:4] + parts[1][4:8]
    start(score_copies())
    out_ref[0] = grads

    def sent(s, carry):
        for p, way in enumerate(WAYS):
            k = s * 2 + p
            core_copy(k).wait_send()
            for copy in copies(k, way, 0) + copies(k, way, 1):
                copy.wait_send()
        return carry

    lax.fori_loop(0, SEQS, sent, 0)
    for copy in spread(0) + spread(1) + query_copies():
        copy.wait_send()
    for copy in score_copies():
        copy.wait_recv()
    total = sbuf[0]
    for q in range(1, 16):
        total = total + sbuf[q]
    out_ref[1] = total * (1.0 / 64.0)
    for copy in score_copies():
        copy.wait_send()


def unpack(packed, grads_ref, scores_ref):
    for h in range(2):
        grads_ref[:, pl.ds(h * 128, 128)] = packed[0, h * 4 : h * 4 + 4]
    scores_ref[...] = packed[1, 0:4, 0:8]


def on_device(hidden_train, outgrad_train, hidden_query, outgrad_query, proj_in, proj_out):
    anywhere = pl.BlockSpec(memory_space=pl.ANY)
    vmem = pl.BlockSpec(memory_space=pltpu.VMEM)
    f32, bf16 = jnp.float32, jnp.bfloat16
    dma = pltpu.SemaphoreType.DMA
    packed = pl.pallas_call(
        kernel,
        out_shape=jax.ShapeDtypeStruct((2, 8, 128), f32),
        in_specs=[anywhere] * 6,
        out_specs=vmem,
        scratch_shapes=[
            pltpu.VMEM((CHUNKS, ROWS, 1792), bf16),
            pltpu.VMEM((CHUNKS, ROWS, 512), bf16),
            pltpu.VMEM((128, 2304), bf16),
            pltpu.VMEM((CHUNKS, ROWS, 128), f32),
            pltpu.VMEM((CHUNKS, HALF, 128), f32),
            pltpu.VMEM((CHUNKS, HALF, 128), f32),
            pltpu.VMEM((CHUNKS * OWN, 128), f32),
            pltpu.VMEM((64, 128), f32),
            pltpu.VMEM((2, 128, 128), f32),
            pltpu.VMEM((2, 15, 8, 128), f32),
            pltpu.VMEM((8, 8, 128), f32),
            pltpu.VMEM((16, 8, 128), f32),
            dma((2 + CHUNKS * 4,)),
            dma((CHUNKS,)),
            dma((CHUNKS,)),
            dma((CHUNKS, 8)),
            dma((CHUNKS, 8)),
            dma((2, 15)),
            dma((2, 15)),
            dma((7,)),
            dma((7,)),
            dma((15,)),
            dma((15,)),
        ],
        compiler_params=pltpu.CompilerParams(
            collective_id=0, has_side_effects=True, vmem_limit_bytes=56 * 2**20
        ),
    )(
        *(
            a.reshape(a.shape[0], 2, 2, HALF, a.shape[2])
            for a in (hidden_train, outgrad_train, hidden_query, outgrad_query)
        ),
        proj_in.T,
        proj_out.T,
    )
    return pl.pallas_call(
        unpack,
        out_shape=(jax.ShapeDtypeStruct((4, 256), f32), jax.ShapeDtypeStruct((4, 8), f32)),
        in_specs=[vmem],
        out_specs=(vmem, vmem),
    )(packed)


def solution(mesh):
    placed = (
        P("dp", None, "tensor"),
        P("dp", None, "tensor"),
        P("dp", None, "tensor"),
        P("dp", None, "tensor"),
        P("tensor", None),
        P("tensor", None),
    )
    return jax.shard_map(
        on_device,
        mesh=mesh,
        in_specs=placed,
        out_specs=(P("dp", "tensor"), P("dp", None)),
        check_vma=False,
    )
```
